512 devices in a mesh: vox: 16 (over x, y_hi, core), vf: 32 (over y_lo, z).
Axes of the slice: x: 4, y: 8 (y_hi: 2, y_lo: 4; y = y_hi * 4 + y_lo), z: 8, core: 2. Of those that a mesh axis runs over, the one named last changes fastest.
Arguments:
- latents: bfloat16 [96, 1024, 1152], P('vf', 'vox'), may hold values from -6 to 6
- block_mask: int32 [96, 16, 32], P('vf', 'vox'), may hold values from 0 to 1, as said below
- occupancy: bfloat16 [32, 64, 512], P('vox'), may hold values from -6 to 6
- temporal_qkv: bfloat16 [1152, 1728], P('vox'), may hold values from -0.1875 to 0.1875
- temporal_out: bfloat16 [576, 1152], P('vox'), may hold values from -0.25 to 0.25
- cross_query: bfloat16 [1152, 576], P('vox'), may hold values from -0.1875 to 0.1875
- cross_keyval: bfloat16 [512, 1152], P('vox'), may hold values from -0.25 to 0.25
- cross_out: bfloat16 [576, 1152], P('vox'), may hold values from -0.25 to 0.25
Outputs:
- mixed_latents: bfloat16 [96, 1024, 1152], P('vf', 'vox')
The draws below stay inside these ranges and needn't reach their ends.
Inputs may be any that keep to these rules, and one draw needn't show every extreme that they name: `block_mask`: every tile (r, b) attends between 1 and 8 voxel blocks, and some tile attends exactly 8.
All inputs are finite; a program needn't handle non-finite values.
Results may differ from the reference program's by a relative error of at most 0.0057.
Values may be sent and summed in bfloat16 or wider, within the bound.
No kernel may reach another device: no remote copies, remote signals or barrier semaphores. Data moves between devices by JAX's collectives and lax.ppermute only.
A program may use at most 128 MiB of HBM per device.

```python
import jax
import jax.numpy as jnp
from jax import lax

D = 1152
HEADS = 8
INNER = 576
C = 512
VIEWS = 6
P_DEV = 64
KB = 64
VFR = 96
PBLK = 16
P_SIZE = 1024
NBLK = 32
MOST = 8


def draw_block_mask(key, part):
    key = jax.random.fold_in(key, 7)
    count_key, second_key, pick_key, order_key = jax.random.split(key, 4)
    first_draw = jax.random.randint(count_key, (VFR, PBLK), 1, MOST + 1)
    second_draw = jax.random.randint(second_key, (VFR, PBLK), 1, MOST + 1)
    counts = (first_draw * second_draw + MOST - 1) // MOST
    picked = jax.random.randint(pick_key, (), 0, VFR * PBLK)
    flat_counts = jnp.where(jnp.arange(VFR * PBLK, dtype=jnp.int32) == picked, MOST, counts.reshape(-1))
    counts = flat_counts.reshape(VFR, PBLK)
    ranking = jax.random.randint(order_key, (VFR, PBLK, NBLK), 0, 1 << 20) * NBLK + jnp.arange(NBLK, dtype=jnp.int32)
    places = jnp.argsort(jnp.argsort(ranking, axis=-1), axis=-1)
    return (places < counts[..., None]).astype(jnp.int32)


def level_of(own_key, extent, shards, low, high):
    level, own = 1.0, jax.random.fold_in(own_key, 6)
    for dim, blocks in shards:
        steps = jnp.exp(jax.random.uniform(jax.random.fold_in(own, dim), (blocks,), jnp.float32, low / len(shards), high / len(shards)))
        level = level * jnp.repeat(steps, extent[dim] // blocks).reshape([-1 if axis == dim else 1 for axis in range(len(extent))])
    return level


def gaussian(rng, shape, width, bound, cuts=(), kind=jnp.bfloat16):
    drawn = jax.random.normal(rng, shape, jnp.float32) * width
    if len(cuts) > 0:
        drawn = level_of(rng, shape, cuts, -0.22, 0.18) * drawn
    return jnp.clip(drawn, min=-bound, max=bound).astype(kind)


def setup_inputs(seed: int = 0) -> dict:
    splits = jax.random.split(jax.random.key(seed), 9)
    latents = gaussian(splits[0], (VFR, P_SIZE, D), 1.0, 6.0, ((0, 32), (1, 16)))
    block_mask = draw_block_mask(jax.random.fold_in(splits[8], 71), 0)
    occupancy = gaussian(splits[2], (NBLK, KB, C), 1.0, 6.0, ((0, 16),))
    temporal_qkv = gaussian(splits[3], (D, 3 * INNER), D ** -0.5, 0.1875, ((0, 16),))
    temporal_out = gaussian(splits[4], (INNER, D), INNER ** -0.5, 0.25, ((0, 16),))
    cross_query = gaussian(splits[5], (D, INNER), D ** -0.5, 0.1875, ((0, 16),))
    cross_keyval = gaussian(splits[6], (C, 2 * INNER), C ** -0.5, 0.25, ((0, 16),))
    cross_out = gaussian(splits[7], (INNER, D), INNER ** -0.5, 0.25, ((0, 16),))
    return {"latents": latents, "block_mask": block_mask, "occupancy": occupancy, "temporal_qkv": temporal_qkv, "temporal_out": temporal_out, "cross_query": cross_query, "cross_keyval": cross_keyval, "cross_out": cross_out}


epsilon = 1e-06

def rms_rows(values):
    return values * lax.rsqrt(lax.optimization_barrier(jnp.mean(values * values, axis=-1, keepdims=True)) + epsilon)

def head_normalize(values, head_count):
    shaped = values.reshape(values.shape[:-1] + (head_count, values.shape[-1] // head_count))
    return rms_rows(shaped).reshape(values.shape)

def slab_project(slab_rows, keyval_weight, head_count):
    block_count, block_width, channels = slab_rows.shape
    projected = jnp.dot(slab_rows.reshape(-1, channels), keyval_weight, preferred_element_type=jnp.float32)
    inner_width = keyval_weight.shape[1] // 2
    key_rows = head_normalize(projected[:, :inner_width], head_count).astype(jnp.bfloat16)
    value_rows = projected[:, inner_width:].astype(jnp.bfloat16)
    return (key_rows.reshape(block_count, block_width, inner_width), value_rows.reshape(block_count, block_width, inner_width))

def temporal_mix(normed, qkv_weight, view_count, head_count, positions):
    projected = jnp.dot(normed, qkv_weight, preferred_element_type=jnp.float32)
    inner_width = qkv_weight.shape[1] // 3
    head_size = inner_width // head_count
    query_rows = head_normalize(projected[:, :inner_width], head_count).astype(jnp.bfloat16)
    key_rows = head_normalize(projected[:, inner_width:2 * inner_width], head_count).astype(jnp.bfloat16)
    value_rows = projected[:, 2 * inner_width:].astype(jnp.bfloat16)

    def to_heads(tensor):
        return tensor.reshape(view_count, -1, positions, head_count, head_size).astype(jnp.float32)
    scores = jnp.einsum('vfphd,vgphd->vphfg', to_heads(query_rows), to_heads(key_rows)) * head_size ** (-0.5)
    exponent = jnp.exp(scores)
    probabilities = (exponent / lax.optimization_barrier(jnp.sum(exponent, axis=-1, keepdims=True))).astype(jnp.bfloat16)
    mixed = jnp.einsum('vphfg,vgphd->vfphd', probabilities.astype(jnp.float32), to_heads(value_rows))
    return mixed.astype(jnp.bfloat16).reshape(-1, inner_width)

def cross_mix(hidden_normed, tile_mask, slab_keys, slab_values, query_weight, head_count, most_blocks):
    tile_count, positions, model_width = hidden_normed.shape
    inner_width = query_weight.shape[1]
    head_size = inner_width // head_count
    query_rows = jnp.dot(hidden_normed.reshape(-1, model_width), query_weight, preferred_element_type=jnp.float32)
    query_rows = head_normalize(query_rows, head_count).astype(jnp.bfloat16)
    query_rows = query_rows.reshape(tile_count, positions, head_count, head_size)
    blocks = slab_keys.shape[0]
    block_width = slab_keys.shape[1]
    ranking = tile_mask * blocks + (blocks - 1 - jnp.arange(blocks, dtype=jnp.int32))[None, :]
    chosen = lax.top_k(ranking, most_blocks)[1].astype(jnp.int32)
    live_blocks = jnp.take_along_axis(tile_mask, chosen, axis=1)
    picked_keys = slab_keys[chosen].reshape(tile_count, most_blocks * block_width, head_count, head_size)
    picked_values = slab_values[chosen].reshape(tile_count, most_blocks * block_width, head_count, head_size)
    key_live = jnp.repeat(live_blocks, block_width, axis=1).astype(jnp.float32)
    scores = jnp.einsum('tphd,tkhd->thpk', query_rows.astype(jnp.float32), picked_keys.astype(jnp.float32)) * head_size ** (-0.5)
    exponent = jnp.exp(scores) * key_live[:, None, None, :]
    probabilities = (exponent / lax.optimization_barrier(jnp.sum(exponent, axis=-1, keepdims=True))).astype(jnp.bfloat16)
    mixed = jnp.einsum('thpk,tkhd->tphd', probabilities.astype(jnp.float32), picked_values.astype(jnp.float32))
    return mixed.astype(jnp.bfloat16).reshape(-1, inner_width)

def reference(latents, block_mask, occupancy, temporal_qkv, temporal_out, cross_query, cross_keyval, cross_out):
    slab_keys, slab_values = slab_project(occupancy, cross_keyval, HEADS)
    blocks_first = latents.reshape(VFR, PBLK, P_DEV, D).transpose(1, 0, 2, 3)
    masks_first = block_mask.transpose(1, 0, 2)

    def one_block(block_pair):
        block_rows, tile_mask = block_pair
        flat_rows = block_rows.reshape(-1, D)
        normed = rms_rows(flat_rows.astype(jnp.float32)).astype(jnp.bfloat16)
        temporal_mixed = temporal_mix(normed, temporal_qkv, VIEWS, HEADS, P_DEV)
        hidden = (flat_rows.astype(jnp.float32) + jnp.dot(temporal_mixed, temporal_out, preferred_element_type=jnp.float32)).astype(jnp.bfloat16)
        hidden_normed = rms_rows(hidden.astype(jnp.float32)).astype(jnp.bfloat16).reshape(VFR, P_DEV, D)
        crossed = cross_mix(hidden_normed, tile_mask, slab_keys, slab_values, cross_query, HEADS, MOST)
        result = (hidden.astype(jnp.float32) + jnp.dot(crossed, cross_out, preferred_element_type=jnp.float32)).astype(jnp.bfloat16)
        return result.reshape(VFR, P_DEV, D)
    stacked = lax.map(one_block, (blocks_first, masks_first))
    return stacked.transpose(1, 0, 2, 3).reshape(VFR, P_SIZE, D)
```

```python
import functools

import jax
import jax.numpy as jnp
from jax import lax
from jax.experimental import pallas as pl
from jax.experimental.pallas import tpu as pltpu
from jax.sharding import Mesh
from jax.sharding import PartitionSpec as P

HEADS = 8
HEAD = 72
INNER = 576
WIDTH = 1152
CHANNELS = 512
EPS = 1e-06
SCALE = HEAD ** (-0.5)
BF = jnp.bfloat16
F32 = jnp.float32

OUT_AT, CO_AT, KV_AT, PACK = 128, 176, 224, 256
CQ_LANE = 512
VMEM = 60 * 1024 * 1024


def mm(a, b):
    return lax.dot_general(a, b, (((1,), (0,)), ((), ())), preferred_element_type=F32)


def mm_nt(a, b):
    return lax.dot_general(a, b, (((1,), (1,)), ((), ())), preferred_element_type=F32)


def iota(shape, dim):
    return lax.broadcasted_iota(jnp.int32, shape, dim)


def onehot(hit):
    return jnp.where(hit, 1.0, 0.0).astype(BF)


def split_mm(a, b):
    high = a.astype(BF)
    low = (a - high.astype(F32)).astype(BF)
    return mm(high, b) + mm(low, b)


def head_normalize(values):
    width = values.shape[1]
    gather = onehot(iota((width, 128), 0) // HEAD == iota((width, 128), 1))
    spread = onehot(iota((128, width), 1) // HEAD == iota((128, width), 0))
    mean = split_mm(values * values, gather) * (1.0 / HEAD)
    return values * split_mm(lax.rsqrt(mean + EPS), spread)


def rms_rows(values):
    return values * lax.rsqrt(jnp.mean(values * values, axis=-1, keepdims=True) + EPS)


def head_masked(rows):
    head = iota(rows.shape, 1) // HEAD
    return jnp.concatenate([jnp.where(head == h, rows, 0.0).astype(BF) for h in range(HEADS)], axis=0)


def head_merged(rows, count):
    head = iota((count, INNER), 1) // HEAD
    total = jnp.where(head == 0, rows[:count], 0.0)
    for h in range(1, HEADS):
        total = jnp.where(head == h, rows[h * count:(h + 1) * count], total)
    return total


def pack_kernel(occ_ref, cq_ref, out_ref, co_ref, kv_ref, packed_ref):
    packed_ref[...] = jnp.zeros(packed_ref.shape, BF)
    to = iota((CHANNELS, CHANNELS), 1)
    yh, x, c, r = to // 256, (to // 64) % 4, (to // 32) % 2, to % 32
    spread = onehot(iota((CHANNELS, CHANNELS), 0) == (x * 4 + yh * 2 + c) * 32 + r)
    packed_ref[0:128, 0:CHANNELS] = mm(occ_ref[...], spread).astype(BF)
    packed_ref[0:72, CQ_LANE:CQ_LANE + INNER] = cq_ref[...]
    packed_ref[OUT_AT:OUT_AT + 36, :] = out_ref[...]
    packed_ref[CO_AT:CO_AT + 36, :] = co_ref[...]
    packed_ref[KV_AT:KV_AT + 32, :] = kv_ref[...]


def send_kernel(lat_ref, sent_ref):
    to, src = iota((256, 192), 0), iota((256, 192), 1)
    j, i, p = to // 16, (to // 4) % 4, to % 4
    pick = onehot((src == i * 64 + j * 4 + p) & (i < 3))
    sent_ref[...] = mm(pick, lat_ref[...]).astype(BF)


def prep_kernel(rows_ref, index_ref, normed_ref):
    to, src = iota((192, 256), 0), iota((192, 256), 1)
    pick = onehot(src == (to // 12) * 16 + to % 12)
    rows = mm(pick, rows_ref[...])
    normed = rms_rows(rows).astype(BF)
    for k in range(4):
        spread = onehot(iota((WIDTH, 384), 0) == index_ref[:, k * 384:(k + 1) * 384])
        normed_ref[:, k * 384:(k + 1) * 384] = mm(normed, spread).astype(BF)


def temporal_kernel(normed_ref, a4_ref, a8_ref, b4_ref, b8_ref, mixed_ref):
    projected = None
    for k, w_ref in enumerate((a4_ref, a8_ref, b4_ref, b8_ref)):
        term = mm(normed_ref[:, k * 384:k * 384 + 288], w_ref[...])
        projected = term if projected is None else projected + term
    both = head_normalize(projected[:, :2 * INNER])
    query = both[:, :INNER]
    key = both[:, INNER:].astype(BF)
    value = projected[:, 2 * INNER:].astype(BF)
    live = iota((HEADS * 64, 64), 0) % 4 == iota((HEADS * 64, 64), 1) % 4
    mixed = []
    for view in range(3):
        rows = slice(view * 64, view * 64 + 64)
        scores = mm_nt(head_masked(query[rows]), key[rows]) * SCALE
        exponent = jnp.where(live, jnp.exp(scores), 0.0)
        weights = (exponent / jnp.sum(exponent, axis=-1, keepdims=True)).astype(BF)
        mixed.append(head_merged(mm(weights, value[rows]), 64).astype(BF))
    to, src = iota((256, 192), 0), iota((256, 192), 1)
    pick = onehot((src == (to // 16) * 12 + to % 16) & (to % 16 < 12))
    mixed_ref[...] = mm(pick, jnp.concatenate(mixed, axis=0)).astype(BF)


def slab_kernel(yh_ref, a_ref, b_ref, key_ref, value_ref):
    wa = a_ref[:, KV_AT:KV_AT + 32, :].reshape(256, WIDTH)
    wb = b_ref[:, KV_AT:KV_AT + 32, :].reshape(256, WIDTH)
    first = yh_ref[0] == 0
    w0 = jnp.where(first, wa, wb)
    w1 = jnp.where(first, wb, wa)
    for side, ref in enumerate((a_ref, b_ref)):
        for part in range(4):
            occ = ref[2 * part:2 * part + 2, 0:128, 0:CHANNELS].reshape(256, CHANNELS)
            projected = mm(occ[:, :256], w0) + mm(occ[:, 256:], w1)
            rows = slice(side * 1024 + part * 256, side * 1024 + part * 256 + 256)
            key_ref[rows, :] = head_normalize(projected[:, :INNER]).astype(BF)
            value_ref[rows, :] = projected[:, INNER:].astype(BF)


def cross_kernel(ids_ref, lat_ref, mixed_ref, live_ref, cols36_ref, cols72_ref, a_ref, b_ref,
                 key_ref, value_ref, result_ref):
    to, src = iota((192, 256), 0), iota((192, 256), 1)
    i, j, p = to // 64, (to % 64) // 4, to % 4
    pick = onehot(src == j * 16 + i * 4 + p)
    mixed = mm(pick, mixed_ref[...]).astype(BF)
    spread36 = onehot(iota((INNER, 768), 0) == cols36_ref[...])

    def out_project(rows, at):
        spread = mm(rows, spread36).astype(BF)
        return mm(spread[:, :384], a_ref[:, at:at + 48, :].reshape(384, WIDTH)) + mm(
            spread[:, 384:], b_ref[:, at:at + 48, :].reshape(384, WIDTH)
        )

    hidden = (lat_ref[...].astype(F32) + out_project(mixed, OUT_AT)).astype(BF)
    normed = rms_rows(hidden.astype(F32)).astype(BF)
    query = None
    for side, ref in enumerate((a_ref, b_ref)):
        spread72 = onehot(iota((WIDTH, 640), 0) == cols72_ref[:, side * 640:side * 640 + 640])
        columns = mm(normed, spread72).astype(BF)
        term = mm(columns, ref[:, 0:80, CQ_LANE:CQ_LANE + INNER].reshape(640, INNER))
        query = term if query is None else query + term
    query = head_normalize(query)
    crossed = []
    for tile in range(3):
        rows = slice(tile * 64, tile * 64 + 64)
        picked = [pl.ds(pl.multiple_of(ids_ref[tile, s] * 64, 64), 64) for s in range(8)]
        keys = jnp.concatenate([key_ref[at, :] for at in picked], axis=0)
        values = jnp.concatenate([value_ref[at, :] for at in picked], axis=0)
        scores = mm_nt(head_masked(query[rows]), keys) * SCALE
        exponent = jnp.exp(scores) * live_ref[tile:tile + 1, :]
        weights = (exponent / jnp.sum(exponent, axis=-1, keepdims=True)).astype(BF)
        crossed.append(head_merged(mm(weights, values), 64).astype(BF))
    crossed = jnp.concatenate(crossed, axis=0)
    result_ref[...] = (hidden.astype(F32) + out_project(crossed, CO_AT)).astype(BF)


def call(kernel, shapes, count, scalars=(), flops=0, size=0):
    memory = [pltpu.SMEM if n in scalars else pltpu.VMEM for n in range(count)]
    return pl.pallas_call(
        kernel,
        out_shape=shapes,
        in_specs=[pl.BlockSpec(memory_space=m) for m in memory],
        out_specs=jax.tree.map(lambda _: pl.BlockSpec(memory_space=pltpu.VMEM), shapes),
        compiler_params=pltpu.CompilerParams(vmem_limit_bytes=VMEM),
        cost_estimate=pl.CostEstimate(flops=flops, bytes_accessed=size, transcendentals=0),
    )


def after(value, *others):
    return lax.optimization_barrier((value,) + others)[0]


SWAP = [(0, 1), (1, 0)]
STEPS = (0, 1, 3, 2)


def shift(block, step):
    return lax.ppermute(block, "x", [(i, (i + step) % 4) for i in range(4)])


def columns_of(slots, order, rows, size, pad):
    place = jnp.arange(pad, dtype=jnp.int32)
    parts = []
    for x, yh, c in order:
        start = ((x * 2 + yh) * 2 + c) * rows
        parts.append(jnp.where(place < rows, start + place, -1))
    flat = jnp.concatenate(parts)
    return flat.reshape(1, -1) if size is None else flat


def shards(latents, block_mask, occupancy, temporal_qkv, temporal_out, cross_query, cross_keyval, cross_out):
    x, yh, c = lax.axis_index("x"), lax.axis_index("yh"), lax.axis_index("c")
    shape = jax.ShapeDtypeStruct
    lat = latents.reshape(192, WIDTH)

    qkv_b = lax.ppermute(temporal_qkv, "yh", SWAP)
    qkv_a4 = jnp.stack([temporal_qkv] + [shift(temporal_qkv, s) for s in STEPS[1:]])
    sent = call(send_kernel, shape((256, WIDTH), BF), 1)(lat)
    time_rows = lax.all_to_all(
        sent.reshape(16, 16, WIDTH), ("l", "z"), split_axis=0, concat_axis=0, tiled=True
    ).reshape(256, WIDTH)
    qkv_b4 = jnp.stack([qkv_b] + [shift(qkv_b, s) for s in STEPS[1:]])
    qkv_a8 = lax.ppermute(qkv_a4, "c", SWAP)
    qkv_b8 = lax.ppermute(qkv_b4, "c", SWAP)

    packed = call(pack_kernel, shape((PACK, WIDTH), BF), 5)(
        occupancy.reshape(128, CHANNELS), cross_query, temporal_out, cross_out, cross_keyval
    )
    packed_b = lax.ppermute(after(packed, qkv_b, qkv_a4), "yh", SWAP)
    rest_a = lax.all_gather(packed, ("x", "c"), axis=0, tiled=False)
    rest_b = lax.all_gather(packed_b, ("x", "c"), axis=0, tiled=False)

    place = jnp.arange(384, dtype=jnp.int32)
    steps = jnp.array(STEPS, jnp.int32)
    source_x = (x - steps[jnp.minimum(place // 72, 3)] + 4) % 4
    index = []
    for dy, dc in ((0, 0), (0, 1), (1, 0), (1, 1)):
        start = ((source_x * 2 + (yh ^ dy)) * 2 + (c ^ dc)) * 72
        index.append(jnp.where(place < 288, start + place % 72, -1))
    index = jnp.concatenate(index).reshape(1, 1536)
    normed = call(prep_kernel, shape((192, 1536), BF), 2)(time_rows, index)
    mixed = call(temporal_kernel, shape((256, INNER), BF), 5)(
        normed, *[w.reshape(288, 1728) for w in (qkv_a4, qkv_a8, qkv_b4, qkv_b8)]
    )
    mixed_home = lax.all_to_all(
        mixed.reshape(16, 16, INNER), ("l", "z"), split_axis=0, concat_axis=0, tiled=True
    ).reshape(256, INNER)

    def columns(rows, pad):
        place = jnp.arange(16 * pad, dtype=jnp.int32)
        slot, row = place // pad, place % pad
        side, sx, sc = slot // 8, (slot // 2) % 4, slot % 2
        start = ((sx * 2 + (yh ^ side)) * 2 + sc) * rows
        return jnp.where(row < rows, start + row, -1).reshape(1, 16 * pad)

    mask = block_mask[:, 0, :]
    rank = jnp.cumsum(mask, axis=1) - 1
    block = jnp.arange(32, dtype=jnp.int32)
    vox, half = block // 2, block % 2
    stored = ((((vox // 2) % 2) ^ yh) * 8 + (vox // 4) * 2 + vox % 2) * 2 + half
    chosen = (rank[:, :, None] == jnp.arange(8, dtype=jnp.int32)) & (mask[:, :, None] > 0)
    ids = jnp.sum(jnp.where(chosen, stored[None, :, None], 0), axis=1).astype(jnp.int32)
    live = jnp.repeat(jnp.any(chosen, axis=1), 64, axis=1).astype(F32)

    keys, values = call(slab_kernel, (shape((2048, INNER), BF),) * 2, 3, scalars=(0,))(
        yh.reshape(1).astype(jnp.int32), rest_a, rest_b
    )
    result = call(cross_kernel, shape((192, WIDTH), BF), 10, scalars=(0,))(
        ids, lat, mixed_home, live, columns(36, 48), columns(72, 80), rest_a, rest_b, keys, values
    )
    return result.reshape(latents.shape)


def solution(mesh):
    split = Mesh(mesh.devices.reshape(4, 2, 2, 2, 2, 8), ("x", "yh", "c", "g", "l", "z"))
    vox, vf = ("x", "yh", "c"), ("g", "l", "z")
    return jax.shard_map(
        shards,
        mesh=split,
        in_specs=(
            P(vf, vox, None),
            P(vf, vox, None),
            P(vox, None, None),
            P(vox, None),
            P(vox, None),
            P(vox, None),
            P(vox, None),
            P(vox, None),
        ),
        out_specs=P(vf, vox, None),
        check_vma=False,
    )
```

```python
import functools

import jax
import jax.numpy as jnp
from jax import lax
from jax.experimental import pallas as pl
from jax.experimental.pallas import tpu as pltpu
from jax.sharding import Mesh
from jax.sharding import PartitionSpec as P

HEADS = 8
HEAD = 72
INNER = 576
HALF = 288
WIDTH = 1152
CHANNELS = 512
EPS = 1e-06
SCALE = HEAD ** (-0.5)
BF = jnp.bfloat16
F32 = jnp.float32

PACK = 896
REST, SLAB, SHARE = 144, 128, 272


def mm(a, b):
    return lax.dot_general(a, b, (((1,), (0,)), ((), ())), preferred_element_type=F32)


def mm_nt(a, b):
    return lax.dot_general(a, b, (((1,), (1,)), ((), ())), preferred_element_type=F32)


def iota(shape, dim):
    return lax.broadcasted_iota(jnp.int32, shape, dim)


def onehot(hit):
    return jnp.where(hit, 1.0, 0.0).astype(BF)


def split_mm(a, b):
    high = a.astype(BF)
    low = (a - high.astype(F32)).astype(BF)
    return mm(high, b) + mm(low, b)


def head_normalize(values):
    width = values.shape[1]
    gather = onehot(iota((width, 128), 0) // HEAD == iota((width, 128), 1))
    spread = onehot(iota((128, width), 1) // HEAD == iota((128, width), 0))
    mean = split_mm(values * values, gather) * (1.0 / HEAD)
    return values * split_mm(lax.rsqrt(mean + EPS), spread)


def rms_rows(values):
    return values * lax.rsqrt(jnp.mean(values * values, axis=-1, keepdims=True) + EPS)


def head_masked(rows):
    head = iota(rows.shape, 1) // HEAD
    return jnp.concatenate([jnp.where(head == h, rows, 0.0).astype(BF) for h in range(4)], axis=0)


def head_merged(rows, count):
    head = iota((count, HALF), 1) // HEAD
    total = rows[:count]
    for h in range(1, 4):
        total = jnp.where(head == h, rows[h * count:(h + 1) * count], total)
    return total.astype(BF)


def first_kernel(l_ref, qkv_ref, occ_ref, kv_ref, lat_ref, cq_ref, out_ref, co_ref,
                 packed_ref, own_ref, share_ref, sent_ref):
    share_ref[...] = jnp.zeros(share_ref.shape, BF)
    rest = jnp.concatenate([out_ref[...], co_ref[...]], axis=0)
    share_ref[0:72, :] = rest[:, 0:PACK]
    share_ref[72:144, 0:256] = rest[:, PACK:]
    share_ref[72:144, 256:256 + INNER] = cq_ref[...]
    share_ref[REST:, 0:CHANNELS] = occ_ref[...]
    for q in range(4):
        at = slice(REST + 32 * q, REST + 32 * q + 32)
        share_ref[at, CHANNELS:CHANNELS + HALF] = kv_ref[:, q * HALF:(q + 1) * HALF]
    packed_ref[0:SHARE, :] = share_ref[...]
    packed_ref[SHARE:, 3 * HALF:] = jnp.zeros((72, PACK - 3 * HALF), BF)
    first = l_ref[0] == 0
    for n in range(3):
        low = qkv_ref[:, n * INNER:n * INNER + HALF]
        high = qkv_ref[:, n * INNER + HALF:(n + 1) * INNER]
        own_ref[:, n * HALF:(n + 1) * HALF] = jnp.where(first, low, high)
        packed_ref[SHARE:, n * HALF:(n + 1) * HALF] = jnp.where(first, high, low)
    to, src = iota((192, 192), 0), iota((192, 192), 1)
    pick = onehot(src == (to // 8) % 3 * 64 + to // 24 * 8 + to % 8)
    rows = mm(pick, lat_ref[...]).astype(BF)
    sent_ref[0:192, :] = rows
    sent_ref[192:384, :] = rows


def prep_kernel(rows_ref, index_ref, own_ref, swapped_ref, normed_ref, qkv_ref, share_ref):
    share_ref[...] = swapped_ref[0:SHARE, :]
    qkv_ref[0] = own_ref[...]
    qkv_ref[1] = swapped_ref[SHARE:, 0:3 * HALF]
    normed = rms_rows(rows_ref[...].astype(F32)).astype(BF)
    for at in range(0, 1280, 256):
        spread = onehot(iota((WIDTH, 256), 0) == index_ref[:, at:at + 256])
        normed_ref[:, at:at + 256] = mm(normed, spread).astype(BF)


def temporal_kernel(normed_ref, own_ref, other_ref, mixed_ref):
    projected = mm(normed_ref[:, 0:INNER], own_ref[...]) + mm(
        normed_ref[:, 640:640 + INNER], other_ref[...]
    )
    both = head_normalize(projected[:, :INNER])
    query = both[:, :HALF]
    key = both[:, HALF:].astype(BF)
    value = projected[:, INNER:].astype(BF)
    live = iota((512, 128), 0) % 8 == iota((512, 128), 1) % 8
    for view in range(3):
        rows = slice(view * 128, view * 128 + 128)
        scores = mm_nt(head_masked(query[rows]), key[rows]) * SCALE
        exponent = jnp.where(live, jnp.exp(scores), 0.0)
        weights = (exponent * (1.0 / jnp.sum(exponent, axis=-1, keepdims=True))).astype(BF)
        mixed_ref[rows, :] = head_merged(mm(weights, value[rows]), 128)


def slab_kernel(index_ref, a_ref, b_ref, slab_ref, rows_ref, held_ref, in_sem, out_sem):
    arrivals = []
    for n in range(16):
        at = pl.ds(n % 8 * SHARE + REST, SLAB)
        arrivals.append(
            pltpu.make_async_copy((a_ref, b_ref)[n // 8].at[at], rows_ref.at[pl.ds(n * SLAB, SLAB)], in_sem.at[n])
        )
        arrivals[-1].start()
    order = onehot(iota((CHANNELS, CHANNELS), 0) == index_ref[...])
    gather = onehot(iota((640, 128), 0) // HEAD == iota((640, 128), 1)) * onehot(iota((640, 128), 1) < HEADS)
    spread = onehot(jnp.minimum(iota((128, WIDTH), 1) // HEAD, HEADS) == iota((128, WIDTH), 0))
    for copy in arrivals:
        copy.wait()
    quarters = []
    for q in range(4):
        parts = [rows_ref[n * SLAB + 32 * q:n * SLAB + 32 * q + 32, CHANNELS:CHANNELS + HALF] for n in range(16)]
        quarters.append(jnp.concatenate(parts, axis=0))
    weight = mm(order, jnp.concatenate(quarters, axis=1)).astype(BF)
    copies = []
    for part in range(8):
        rows = pl.ds(part * 256, 256)
        projected = mm(rows_ref[rows, 0:CHANNELS], weight)
        mean = split_mm(projected[:, :640] * projected[:, :640], gather) * (1.0 / HEAD)
        factor = jnp.where(iota((256, 128), 1) < HEADS, lax.rsqrt(mean + EPS), 1.0)
        held_ref[rows, :] = (projected * split_mm(factor, spread)).astype(BF)
        copies.append(pltpu.make_async_copy(held_ref.at[rows], slab_ref.at[rows], out_sem.at[part]))
        copies[-1].start()
    for copy in copies:
        copy.wait()


def cross_kernel(ids_ref, lat_ref, mixed_ref, live_ref, index72_ref, index36_ref, a_ref, b_ref, slab_ref,
                 result_ref, a_held, b_held, picked_ref, out_ref, co_ref, cq_ref, sem):
    weights = []
    for n in range(16):
        at = pl.ds(n % 8 * SHARE, REST)
        held = (a_held, b_held)[n // 8].at[pl.ds(n % 8 * REST, REST)]
        weights.append(pltpu.make_async_copy((a_ref, b_ref)[n // 8].at[at], held, sem.at[24 + n]))
        weights[-1].start()
    blocks = []
    for n in range(24):
        block = pl.ds(pl.multiple_of(ids_ref[n // 8, n % 8] * 64, 64), 64)
        blocks.append(pltpu.make_async_copy(slab_ref.at[block], picked_ref.at[pl.ds(n * 64, 64)], sem.at[n]))
        blocks[-1].start()

    to, src = iota((192, 192), 0), iota((192, 192), 1)
    pick = onehot(src == (to % 64) // 8 * 24 + to // 64 * 8 + to % 8)
    spread36 = onehot(iota((INNER, INNER), 0) == index36_ref[...])
    halves = [mm(pick, mixed_ref[at:at + 192, :]).astype(BF) for at in (0, 192)]
    mixed = mm(halves[0], spread36[:HALF]) + mm(halves[1], spread36[HALF:])
    spread72 = onehot(iota((WIDTH, WIDTH), 0) == index72_ref[...])
    for side, ref in enumerate((a_held, b_held)):
        for j in range(8):
            weights[side * 8 + j].wait()
            to = slice(side * HALF + j * 36, side * HALF + j * 36 + 36)
            at = j * 144
            out_ref[to, 0:PACK] = ref[at:at + 36, :]
            co_ref[to, 0:PACK] = ref[at + 36:at + 72, :]
            out_ref[to, PACK:] = ref[at + 72:at + 108, 0:256]
            co_ref[to, PACK:] = ref[at + 108:at + 144, 0:256]
            cq_ref[side * INNER + j * 72:side * INNER + j * 72 + 72, :] = ref[at + 72:at + 144, 256:256 + INNER]
    hidden = (lat_ref[...].astype(F32) + mm(mixed.astype(BF), out_ref[...])).astype(BF)
    normed = rms_rows(hidden.astype(F32)).astype(BF)
    query = head_normalize(mm(mm(normed, spread72).astype(BF), cq_ref[...]))
    query = jnp.concatenate([query, jnp.zeros((192, 64), F32)], axis=1)
    head = iota((64, 640), 1) // HEAD
    value_head = (iota((64, 640), 1) - 64 + HEAD) // HEAD - 1
    crossed = []
    for tile in range(3):
        for copy in blocks[tile * 8:tile * 8 + 8]:
            copy.wait()
        rows = query[tile * 64:tile * 64 + 64]
        masked = jnp.concatenate([jnp.where(head == h, rows, 0.0).astype(BF) for h in range(HEADS)], axis=0)
        keys = slice(tile * 512, tile * 512 + 512)
        scores = mm_nt(masked, picked_ref[keys, 0:640]) * SCALE
        exponent = jnp.exp(scores) * live_ref[tile:tile + 1, :]
        weights = (exponent * (1.0 / jnp.sum(exponent, axis=-1, keepdims=True))).astype(BF)
        mixed = mm(weights, picked_ref[keys, 512:WIDTH])
        total = mixed[:64]
        for h in range(1, HEADS):
            total = jnp.where(value_head == h, mixed[h * 64:h * 64 + 64], total)
        crossed.append(total)
    crossed = jnp.concatenate(crossed, axis=0)[:, 64:].astype(BF)
    columns = mm(crossed, spread36).astype(BF)
    result_ref[...] = (hidden.astype(F32) + mm(columns, co_ref[...])).astype(BF)


def call(kernel, shapes, count, scalars=(), hbm=(), out_hbm=False, scratch=(), us=1, vmem=60):
    memory = [pltpu.SMEM if n in scalars else pl.ANY if n in hbm else pltpu.VMEM for n in range(count)]
    out_memory = pl.ANY if out_hbm else pltpu.VMEM
    return pl.pallas_call(
        kernel,
        out_shape=shapes,
        in_specs=[pl.BlockSpec(memory_space=m) for m in memory],
        out_specs=jax.tree.map(lambda _: pl.BlockSpec(memory_space=out_memory), shapes),
        scratch_shapes=scratch,
        compiler_params=pltpu.CompilerParams(vmem_limit_bytes=vmem * 1024 * 1024),
        cost_estimate=pl.CostEstimate(flops=us * 1150000000, bytes_accessed=us * 1000000, transcendentals=0),
    )


def after(values, *others):
    count = len(values)
    return lax.optimization_barrier(tuple(values) + others)[:count]


SWAP = [(0, 1), (1, 0)]
STEPS = (0, 1, 3, 2)


def along_x(block):
    return [block] + [lax.ppermute(block, "x", [(i, (i + s) % 4) for i in range(4)]) for s in STEPS[1:]]


def across_core(blocks):
    stacked = jnp.stack(blocks)
    return stacked, lax.ppermute(stacked, "c", SWAP)


def places(device, sides, rows, pad):
    place = jnp.arange(sides * pad, dtype=jnp.int32)
    side, row = place // pad, place % pad
    x, yh, c = device(side, row // rows)
    start = ((x * 2 + yh) * 2 + c) * rows
    return jnp.where(row < 16 // sides * rows, start + row % rows, -1).reshape(1, sides * pad)


def shards(latents, block_mask, occupancy, temporal_qkv, temporal_out, cross_query, cross_keyval, cross_out):
    x, yh, c, l = (lax.axis_index(name) for name in ("x", "yh", "c", "l"))
    shape = jax.ShapeDtypeStruct
    lat = latents.reshape(192, WIDTH)

    def by_step(side, j):
        return (x - jnp.array(STEPS, jnp.int32)[jnp.minimum(j // 2, 3)] + 4) % 4, yh ^ (j % 2), c ^ side

    def by_x_core(side, j):
        return j // 2, yh ^ side, j % 2

    packed, qkv, share, sent = call(
        first_kernel,
        (shape((SHARE + 72, PACK), BF), shape((72, 3 * HALF), BF), shape((SHARE, PACK), BF), shape((384, WIDTH), BF)),
        8, scalars=(0,), us=3,
    )(
        l.reshape(1).astype(jnp.int32), temporal_qkv, occupancy.reshape(128, CHANNELS), cross_keyval,
        lat, cross_query, temporal_out, cross_out,
    )
    swapped = lax.ppermute(packed, ("yh", "g", "l"), [(y, 7 - y) for y in range(8)])
    share_a = lax.all_gather(share, ("x", "c"), axis=0, tiled=True)
    time_rows = lax.all_to_all(
        sent.reshape(16, 24, WIDTH), ("l", "z"), split_axis=0, concat_axis=0, tiled=True
    ).reshape(384, WIDTH)
    normed, qkv_both, share_swapped = call(
        prep_kernel,
        (shape((384, 1280), BF), shape((2, 72, 3 * HALF), BF), shape((SHARE, PACK), BF)),
        4, us=3, vmem=24,
    )(time_rows, places(by_step, 2, 72, 640), qkv, swapped)
    share_b = lax.all_gather(share_swapped, ("x", "c"), axis=0, tiled=True)
    qkv_own, qkv_other = across_core(along_x(qkv_both))
    mixed = call(temporal_kernel, shape((384, HALF), BF), 3, us=5, vmem=24)(
        normed, qkv_own.reshape(INNER, 3 * HALF), qkv_other.reshape(INNER, 3 * HALF)
    )
    mixed_home = lax.all_to_all(
        mixed.reshape(16, 24, HALF), ("l", "z"), split_axis=0, concat_axis=0, tiled=True
    ).reshape(384, HALF)

    mask = block_mask[:, 0, :]
    rank = jnp.cumsum(mask, axis=1) - 1
    block = jnp.arange(32, dtype=jnp.int32)
    vox, half = block // 2, block % 2
    stored = ((vox // 2 % 2 ^ yh) * 8 + vox // 4 * 2 + vox % 2) * 2 + half
    chosen = (rank[:, :, None] == jnp.arange(8, dtype=jnp.int32)) & (mask[:, :, None] > 0)
    ids = jnp.sum(jnp.where(chosen, stored[None, :, None], 0), axis=1).astype(jnp.int32)
    live = jnp.repeat(jnp.any(chosen, axis=1), 64, axis=1).astype(F32)

    keys_values = call(
        slab_kernel, shape((2048, WIDTH), BF), 3, hbm=(1, 2), out_hbm=True, us=10,
        scratch=[
            pltpu.VMEM((2048, PACK), BF),
            pltpu.VMEM((2048, WIDTH), BF),
            pltpu.SemaphoreType.DMA((16,)),
            pltpu.SemaphoreType.DMA((8,)),
        ],
    )(places(by_x_core, 2, 32, 256), share_a, share_b)
    result = call(
        cross_kernel, shape((192, WIDTH), BF), 9, scalars=(0,), hbm=(6, 7, 8), us=10,
        scratch=[
            pltpu.VMEM((WIDTH, PACK), BF),
            pltpu.VMEM((WIDTH, PACK), BF),
            pltpu.VMEM((24 * 64, WIDTH), BF),
            pltpu.VMEM((INNER, WIDTH), BF),
            pltpu.VMEM((INNER, WIDTH), BF),
            pltpu.VMEM((WIDTH, INNER), BF),
            pltpu.SemaphoreType.DMA((40,)),
        ],
    )(
        ids, lat, mixed_home, live, places(by_x_core, 2, 72, INNER), places(by_x_core, 2, 36, HALF),
        share_a, share_b, keys_values,
    )
    return result.reshape(latents.shape)


def solution(mesh):
    split = Mesh(mesh.devices.reshape(4, 2, 2, 2, 2, 8), ("x", "yh", "c", "g", "l", "z"))
    vox, vf = ("x", "yh", "c"), ("g", "l", "z")
    return jax.shard_map(
        shards,
        mesh=split,
        in_specs=(
            P(vf, vox, None),
            P(vf, vox, None),
            P(vox, None, None),
            P(vox, None),
            P(vox, None),
            P(vox, None),
            P(vox, None),
            P(vox, None),
        ),
        out_specs=P(vf, vox, None),
        check_vma=False,
    )
```

```python
import functools

import jax
import jax.numpy as jnp
from jax import lax
from jax.experimental import pallas as pl
from jax.experimental.pallas import tpu as pltpu
from jax.sharding import Mesh
from jax.sharding import PartitionSpec as P

HEADS = 8
HEAD = 72
INNER = 576
HALF = 288
WIDTH = 1152
CHANNELS = 512
EPS = 1e-06
SCALE = HEAD ** (-0.5)
BF = jnp.bfloat16
F32 = jnp.float32

PACK = 896
REST, SLAB, SHARE = 144, 128, 272


def mm(a, b):
    return lax.dot_general(a, b, (((1,), (0,)), ((), ())), preferred_element_type=F32)


def mm_nt(a, b):
    return lax.dot_general(a, b, (((1,), (1,)), ((), ())), preferred_element_type=F32)


def iota(shape, dim):
    return lax.broadcasted_iota(jnp.int32, shape, dim)


def onehot(hit):
    return jnp.where(hit, 1.0, 0.0).astype(BF)


def head_sums(width, count):
    row = iota((width, 128), 0) // HEAD
    return onehot((row == iota((width, 128), 1)) & (row < count))


def head_spread(width, count):
    return onehot(iota((256, width), 0) % 128 == jnp.minimum(iota((256, width), 1) // HEAD, count))


def head_factors(values, sums, count):
    squares = values * values
    high = squares.astype(BF)
    low = (squares - high.astype(F32)).astype(BF)
    mean = (mm(high, sums) + mm(low, sums)) * (1.0 / HEAD)
    factor = jnp.where(iota(mean.shape, 1) < count, lax.rsqrt(mean + EPS), 1.0)
    high = factor.astype(BF)
    return jnp.concatenate([high, (factor - high.astype(F32)).astype(BF)], axis=1)


def head_normalize(values):
    width = values.shape[1]
    count = width // HEAD
    return values * mm(head_factors(values, head_sums(width, count), count), head_spread(width, count))


def rms_rows(values):
    return values * lax.rsqrt(jnp.mean(values * values, axis=-1, keepdims=True) + EPS)


def head_masked(rows):
    head = iota(rows.shape, 1) // HEAD
    return jnp.concatenate([jnp.where(head == h, rows, 0.0).astype(BF) for h in range(4)], axis=0)


def head_merged(rows, count):
    head = iota((count, HALF), 1) // HEAD
    total = rows[:count]
    for h in range(1, 4):
        total = jnp.where(head == h, rows[h * count:(h + 1) * count], total)
    return total.astype(BF)


def first_kernel(l_ref, qkv_ref, occ_ref, kv_ref, cq_ref, out_ref, co_ref, lat_ref, far_ref, own_ref, share_ref, sent_ref):
    share_ref[...] = jnp.zeros(share_ref.shape, BF)
    rest = jnp.concatenate([out_ref[...], co_ref[...]], axis=0)
    share_ref[0:72, :] = rest[:, 0:PACK]
    share_ref[72:144, 0:256] = rest[:, PACK:]
    share_ref[72:144, 256:256 + INNER] = cq_ref[...]
    share_ref[REST:, 0:CHANNELS] = occ_ref[...]
    for q in range(4):
        at = slice(REST + 32 * q, REST + 32 * q + 32)
        share_ref[at, CHANNELS:CHANNELS + HALF] = kv_ref[:, q * HALF:(q + 1) * HALF]
    first = l_ref[0] == 0
    for n in range(3):
        low = qkv_ref[:, n * INNER:n * INNER + HALF]
        high = qkv_ref[:, n * INNER + HALF:(n + 1) * INNER]
        own_ref[:, n * HALF:(n + 1) * HALF] = jnp.where(first, low, high)
        far_ref[:, n * HALF:(n + 1) * HALF] = jnp.where(first, high, low)
    to, src = iota((192, 192), 0), iota((192, 192), 1)
    pick = onehot(src == (to // 8) % 3 * 64 + to // 24 * 8 + to % 8)
    rows = mm(pick, lat_ref[...]).astype(BF)
    sent_ref[0:192, :] = rows
    sent_ref[192:384, :] = rows


def prep_kernel(rows_ref, index_ref, normed_ref):
    normed = rms_rows(rows_ref[...].astype(F32)).astype(BF)
    for at in range(0, 1280, 256):
        spread = onehot(iota((WIDTH, 256), 0) == index_ref[:, at:at + 256])
        normed_ref[:, at:at + 256] = mm(normed, spread).astype(BF)


def temporal_kernel(normed_ref, own_ref, other_ref, mixed_ref):
    projected = mm(normed_ref[:, 0:INNER], own_ref[...]) + mm(
        normed_ref[:, 640:640 + INNER], other_ref[...]
    )
    both = head_normalize(projected[:, :INNER])
    query = both[:, :HALF]
    key = both[:, HALF:].astype(BF)
    value = projected[:, INNER:].astype(BF)
    live = iota((512, 128), 0) % 8 == iota((512, 128), 1) % 8
    for view in range(3):
        rows = slice(view * 128, view * 128 + 128)
        scores = mm_nt(head_masked(query[rows]), key[rows]) * SCALE
        exponent = jnp.where(live, jnp.exp(scores), 0.0)
        weights = (exponent * (1.0 / jnp.sum(exponent, axis=-1, keepdims=True))).astype(BF)
        mixed_ref[rows, :] = head_merged(mm(weights, value[rows]), 128)


def slab_kernel(yh_ref, a_ref, b_ref, slab_ref, rows_ref, held_ref, in_sem, out_sem):
    arrivals = []
    for n in range(16):
        side, x, c = n // 8, n // 2 % 4, n % 2
        yh = yh_ref[0] if side == 0 else 1 - yh_ref[0]
        to = pl.multiple_of((x * 4 + c) * SLAB + yh * (2 * SLAB), SLAB)
        src = (a_ref, b_ref)[side].at[pl.ds(n % 8 * SHARE + REST, SLAB)]
        arrivals.append(pltpu.make_async_copy(src, rows_ref.at[pl.ds(to, SLAB)], in_sem.at[n]))
        arrivals[-1].start()
    sums, spread = head_sums(640, HEADS), head_spread(640, HEADS)
    for copy in arrivals:
        copy.wait()
    quarters = []
    for q in range(4):
        parts = [rows_ref[n * SLAB + 32 * q:n * SLAB + 32 * q + 32, CHANNELS:CHANNELS + HALF] for n in range(16)]
        quarters.append(jnp.concatenate(parts, axis=0))
    weight = jnp.concatenate(quarters, axis=1)
    copies = []
    for part in range(8):
        rows = pl.ds(part * 256, 256)
        projected = mm(rows_ref[rows, 0:CHANNELS], weight)
        keys = projected[:, :640]
        held_ref[rows, 0:640] = (keys * mm(head_factors(keys, sums, HEADS), spread)).astype(BF)
        held_ref[rows, 640:] = projected[:, 640:].astype(BF)
        copies.append(pltpu.make_async_copy(held_ref.at[rows], slab_ref.at[rows], out_sem.at[part]))
        copies[-1].start()
    for copy in copies:
        copy.wait()


def cross_kernel(ids_ref, yh_ref, lat_ref, mixed_ref, live_ref, a_ref, b_ref, slab_ref,
                 result_ref, held_ref, picked_ref, out_ref, co_ref, cq_ref, sem):
    arrivals = []
    for n in range(16):
        yh = yh_ref[0] if n < 8 else 1 - yh_ref[0]
        to = pl.multiple_of(yh * (8 * REST) + n % 8 * REST, REST)
        src = (a_ref, b_ref)[n // 8].at[pl.ds(n % 8 * SHARE, REST)]
        arrivals.append(pltpu.make_async_copy(src, held_ref.at[pl.ds(to, REST)], sem.at[24 + n]))
        arrivals[-1].start()
    blocks = []
    for n in range(24):
        block = pl.ds(pl.multiple_of(ids_ref[n // 8, n % 8] * 64, 64), 64)
        blocks.append(pltpu.make_async_copy(slab_ref.at[block], picked_ref.at[pl.ds(n * 64, 64)], sem.at[n]))
        blocks[-1].start()

    to, src = iota((192, 192), 0), iota((192, 192), 1)
    pick = onehot(src == (to % 64) // 8 * 24 + to // 64 * 8 + to % 8)
    mixed = jnp.concatenate([mm(pick, mixed_ref[at:at + 192, :]) for at in (0, 192)], axis=1).astype(BF)
    for copy in arrivals:
        copy.wait()
    for n in range(16):
        x, yh, c = n // 4, n // 2 % 2, n % 2
        at = (yh * 8 + x * 2 + c) * REST
        to = slice(n * 36, n * 36 + 36)
        out_ref[to, 0:PACK] = held_ref[at:at + 36, :]
        co_ref[to, 0:PACK] = held_ref[at + 36:at + 72, :]
        out_ref[to, PACK:] = held_ref[at + 72:at + 108, 0:256]
        co_ref[to, PACK:] = held_ref[at + 108:at + 144, 0:256]
        cq_ref[n * 72:n * 72 + 72, :] = held_ref[at + 72:at + 144, 256:256 + INNER]
    hidden = (lat_ref[...].astype(F32) + mm(mixed, out_ref[...])).astype(BF)
    normed = rms_rows(hidden.astype(F32)).astype(BF)
    query = head_normalize(mm(normed, cq_ref[...]))
    query = jnp.concatenate([query, jnp.zeros((192, 64), F32)], axis=1)
    head = iota((64, 640), 1) // HEAD
    value_head = (iota((64, 640), 1) - 64 + HEAD) // HEAD - 1
    crossed = []
    for tile in range(3):
        for copy in blocks[tile * 8:tile * 8 + 8]:
            copy.wait()
        rows = query[tile * 64:tile * 64 + 64]
        masked = jnp.concatenate([jnp.where(head == h, rows, 0.0).astype(BF) for h in range(HEADS)], axis=0)
        keys = slice(tile * 512, tile * 512 + 512)
        scores = mm_nt(masked, picked_ref[keys, 0:640]) * SCALE
        exponent = jnp.exp(scores) * live_ref[tile:tile + 1, :]
        weights = (exponent * (1.0 / jnp.sum(exponent, axis=-1, keepdims=True))).astype(BF)
        mixed = mm(weights, picked_ref[keys, 512:WIDTH])
        total = mixed[:64]
        for h in range(1, HEADS):
            total = jnp.where(value_head == h, mixed[h * 64:h * 64 + 64], total)
        crossed.append(total)
    crossed = jnp.concatenate(crossed, axis=0)[:, 64:].astype(BF)
    result_ref[...] = (hidden.astype(F32) + mm(crossed, co_ref[...])).astype(BF)


def call(kernel, shapes, count, scalars=(), hbm=(), out_hbm=False, scratch=(), us=1, vmem=60):
    memory = [pltpu.SMEM if n in scalars else pl.ANY if n in hbm else pltpu.VMEM for n in range(count)]
    out_memory = pl.ANY if out_hbm else pltpu.VMEM
    return pl.pallas_call(
        kernel,
        out_shape=shapes,
        in_specs=[pl.BlockSpec(memory_space=m) for m in memory],
        out_specs=jax.tree.map(lambda _: pl.BlockSpec(memory_space=out_memory), shapes),
        scratch_shapes=scratch,
        compiler_params=pltpu.CompilerParams(vmem_limit_bytes=vmem * 1024 * 1024),
        cost_estimate=pl.CostEstimate(flops=us * 1150000000, bytes_accessed=us * 1000000, transcendentals=0),
    )


def after(values, *others):
    count = len(values)
    return lax.optimization_barrier(tuple(values) + others)[:count]


SWAP = [(0, 1), (1, 0)]
STEPS = (0, 1, 3, 2)


def along_x(block):
    return [block] + [lax.ppermute(block, "x", [(i, (i + s) % 4) for i in range(4)]) for s in STEPS[1:]]


def across_core(blocks):
    stacked = jnp.stack(blocks)
    return stacked, lax.ppermute(stacked, "c", SWAP)


def places(device, rows, pad):
    place = jnp.arange(2 * pad, dtype=jnp.int32)
    side, row = place // pad, place % pad
    x, yh, c = device(side, row // rows)
    start = ((x * 2 + yh) * 2 + c) * rows
    return jnp.where(row < 8 * rows, start + row % rows, -1).reshape(1, 2 * pad)


def shards(latents, block_mask, occupancy, temporal_qkv, temporal_out, cross_query, cross_keyval, cross_out):
    x, yh, c, l = (lax.axis_index(name) for name in ("x", "yh", "c", "l"))
    shape = jax.ShapeDtypeStruct
    lat = latents.reshape(192, WIDTH)

    def by_step(side, j):
        return (x - jnp.array(STEPS, jnp.int32)[jnp.minimum(j // 2, 3)] + 4) % 4, yh ^ (j % 2), c ^ side

    far, qkv, share, sent = call(
        first_kernel,
        (shape((72, 3 * HALF), BF), shape((72, 3 * HALF), BF), shape((SHARE, PACK), BF), shape((384, WIDTH), BF)),
        8, scalars=(0,), us=3,
    )(
        l.reshape(1).astype(jnp.int32), temporal_qkv, occupancy.reshape(128, CHANNELS), cross_keyval,
        cross_query, temporal_out, cross_out, lat,
    )

    def swap(block):
        return lax.ppermute(block, ("yh", "g", "l"), [(y, 7 - y) for y in range(8)])

    qkv_swapped, share_swapped = swap(far), swap(share)
    share_a = lax.all_gather(share, ("x", "c"), axis=0, tiled=True)
    time_rows = lax.all_to_all(
        sent.reshape(16, 24, WIDTH), ("l", "z"), split_axis=0, concat_axis=0, tiled=True
    ).reshape(384, WIDTH)
    own_blocks = along_x(qkv)
    share_swapped, qkv_swapped = after((share_swapped, qkv_swapped), time_rows, *own_blocks)
    normed = call(prep_kernel, shape((384, 1280), BF), 2, us=3, vmem=24)(time_rows, places(by_step, 72, 640))
    share_b = lax.all_gather(share_swapped, ("x", "c"), axis=0, tiled=True)
    pairs = zip(own_blocks, along_x(qkv_swapped))
    qkv_own, qkv_other = across_core([block for pair in pairs for block in pair])
    mixed = call(temporal_kernel, shape((384, HALF), BF), 3, us=5, vmem=24)(
        normed, qkv_own.reshape(INNER, 3 * HALF), qkv_other.reshape(INNER, 3 * HALF)
    )
    mixed_home = lax.all_to_all(
        mixed.reshape(16, 24, HALF), ("l", "z"), split_axis=0, concat_axis=0, tiled=True
    ).reshape(384, HALF)

    mask = block_mask[:, 0, :]
    rank = jnp.cumsum(mask, axis=1) - 1
    block = jnp.arange(32, dtype=jnp.int32)
    chosen = (rank[:, :, None] == jnp.arange(8, dtype=jnp.int32)) & (mask[:, :, None] > 0)
    ids = jnp.sum(jnp.where(chosen, block[None, :, None], 0), axis=1).astype(jnp.int32)
    live = jnp.repeat(jnp.any(chosen, axis=1), 64, axis=1).astype(F32)

    y_hi = yh.reshape(1).astype(jnp.int32)
    keys_values = call(
        slab_kernel, shape((2048, WIDTH), BF), 3, scalars=(0,), hbm=(1, 2), out_hbm=True, us=10,
        scratch=[
            pltpu.VMEM((2048, PACK), BF),
            pltpu.VMEM((2048, WIDTH), BF),
            pltpu.SemaphoreType.DMA((16,)),
            pltpu.SemaphoreType.DMA((8,)),
        ],
    )(y_hi, share_a, share_b)
    result = call(
        cross_kernel, shape((192, WIDTH), BF), 8, scalars=(0, 1), hbm=(5, 6, 7), us=10,
        scratch=[
            pltpu.VMEM((16 * REST, PACK), BF),
            pltpu.VMEM((24 * 64, WIDTH), BF),
            pltpu.VMEM((INNER, WIDTH), BF),
            pltpu.VMEM((INNER, WIDTH), BF),
            pltpu.VMEM((WIDTH, INNER), BF),
            pltpu.SemaphoreType.DMA((40,)),
        ],
    )(ids, y_hi, lat, mixed_home, live, share_a, share_b, keys_values)
    return result.reshape(latents.shape)


def solution(mesh):
    split = Mesh(mesh.devices.reshape(4, 2, 2, 2, 2, 8), ("x", "yh", "c", "g", "l", "z"))
    vox, vf = ("x", "yh", "c"), ("g", "l", "z")
    return jax.shard_map(
        shards,
        mesh=split,
        in_specs=(
            P(vf, vox, None),
            P(vf, vox, None),
            P(vox, None, None),
            P(vox, None),
            P(vox, None),
            P(vox, None),
            P(vox, None),
            P(vox, None),
        ),
        out_specs=P(vf, vox, None),
        check_vma=False,
    )
```

```python
import functools

import jax
import jax.numpy as jnp
from jax import lax
from jax.experimental import pallas as pl
from jax.experimental.pallas import tpu as pltpu
from jax.sharding import Mesh
from jax.sharding import PartitionSpec as P

HEADS = 8
HEAD = 72
INNER = 576
HALF = 288
WIDTH = 1152
CHANNELS = 512
EPS = 1e-06
SCALE = HEAD ** (-0.5)
BF = jnp.bfloat16
F32 = jnp.float32

PACK = 896
REST, SLAB, SHARE = 144, 128, 272


def mm(a, b):
    return lax.dot_general(a, b, (((1,), (0,)), ((), ())), preferred_element_type=F32)


def mm_nt(a, b):
    return lax.dot_general(a, b, (((1,), (1,)), ((), ())), preferred_element_type=F32)


def iota(shape, dim):
    return lax.broadcasted_iota(jnp.int32, shape, dim)


def onehot(hit):
    return jnp.where(hit, 1.0, 0.0).astype(BF)


def head_sums(width, count):
    row = iota((width, 128), 0) // HEAD
    return onehot((row == iota((width, 128), 1)) & (row < count))


def head_spread(width, count):
    return onehot(iota((256, width), 0) % 128 == jnp.minimum(iota((256, width), 1) // HEAD, count))


def head_factors(values, sums, count):
    squares = values * values
    high = squares.astype(BF)
    low = (squares - high.astype(F32)).astype(BF)
    mean = (mm(high, sums) + mm(low, sums)) * (1.0 / HEAD)
    factor = jnp.where(iota(mean.shape, 1) < count, lax.rsqrt(mean + EPS), 1.0)
    high = factor.astype(BF)
    return jnp.concatenate([high, (factor - high.astype(F32)).astype(BF)], axis=1)


def head_normalize(values):
    width = values.shape[1]
    count = width // HEAD
    return values * mm(head_factors(values, head_sums(width, count), count), head_spread(width, count))


def rms_rows(values):
    return values * lax.rsqrt(jnp.mean(values * values, axis=-1, keepdims=True) + EPS)


def head_masked(rows):
    head = iota(rows.shape, 1) // HEAD
    return jnp.concatenate([jnp.where(head == h, rows, 0.0).astype(BF) for h in range(4)], axis=0)


def head_merged(rows, count):
    head = iota((count, HALF), 1) // HEAD
    total = rows[:count]
    for h in range(1, 4):
        total = jnp.where(head == h, rows[h * count:(h + 1) * count], total)
    return total.astype(BF)


def share_kernel(occ_ref, kv_ref, cq_ref, out_ref, co_ref, share_ref):
    share_ref[...] = jnp.zeros(share_ref.shape, BF)
    rest = jnp.concatenate([out_ref[...], co_ref[...]], axis=0)
    share_ref[0:72, :] = rest[:, 0:PACK]
    share_ref[72:144, 0:256] = rest[:, PACK:]
    share_ref[72:144, 256:256 + INNER] = cq_ref[...]
    share_ref[REST:, 0:CHANNELS] = occ_ref[...]
    for q in range(4):
        at = slice(REST + 32 * q, REST + 32 * q + 32)
        share_ref[at, CHANNELS:CHANNELS + HALF] = kv_ref[:, q * HALF:(q + 1) * HALF]


def send_kernel(l_ref, qkv_ref, lat_ref, far_ref, own_ref, sent_ref):
    first = l_ref[0] == 0
    for n in range(3):
        low = qkv_ref[:, n * INNER:n * INNER + HALF]
        high = qkv_ref[:, n * INNER + HALF:(n + 1) * INNER]
        own_ref[:, n * HALF:(n + 1) * HALF] = jnp.where(first, low, high)
        far_ref[:, n * HALF:(n + 1) * HALF] = jnp.where(first, high, low)
    to, src = iota((192, 192), 0), iota((192, 192), 1)
    pick = onehot(src == (to // 8) % 3 * 64 + to // 24 * 8 + to % 8)
    rows = mm(pick, lat_ref[...]).astype(BF)
    sent_ref[0:192, :] = rows
    sent_ref[192:384, :] = rows


def prep_kernel(rows_ref, index_ref, normed_ref):
    normed = rms_rows(rows_ref[...].astype(F32)).astype(BF)
    for at in range(0, 1280, 256):
        spread = onehot(iota((WIDTH, 256), 0) == index_ref[:, at:at + 256])
        normed_ref[:, at:at + 256] = mm(normed, spread).astype(BF)


def temporal_kernel(normed_ref, own_ref, other_ref, mixed_ref):
    projected = mm(normed_ref[:, 0:INNER], own_ref[...]) + mm(
        normed_ref[:, 640:640 + INNER], other_ref[...]
    )
    both = head_normalize(projected[:, :INNER])
    query = both[:, :HALF]
    key = both[:, HALF:].astype(BF)
    value = projected[:, INNER:].astype(BF)
    live = iota((512, 128), 0) % 8 == iota((512, 128), 1) % 8
    for view in range(3):
        rows = slice(view * 128, view * 128 + 128)
        scores = mm_nt(head_masked(query[rows]), key[rows]) * SCALE
        exponent = jnp.where(live, jnp.exp(scores), 0.0)
        weights = (exponent * (1.0 / jnp.sum(exponent, axis=-1, keepdims=True))).astype(BF)
        mixed_ref[rows, :] = head_merged(mm(weights, value[rows]), 128)


def slab_kernel(yh_ref, a_ref, b_ref, slab_ref, rows_ref, held_ref, in_sem, out_sem):
    arrivals = []
    for n in range(16):
        side, x, c = n // 8, n // 2 % 4, n % 2
        yh = yh_ref[0] if side == 0 else 1 - yh_ref[0]
        to = pl.multiple_of((x * 4 + c) * SLAB + yh * (2 * SLAB), SLAB)
        src = (a_ref, b_ref)[side].at[pl.ds(n % 8 * SHARE + REST, SLAB)]
        arrivals.append(pltpu.make_async_copy(src, rows_ref.at[pl.ds(to, SLAB)], in_sem.at[n]))
        arrivals[-1].start()
    sums, spread = head_sums(640, HEADS), head_spread(640, HEADS)
    for copy in arrivals:
        copy.wait()
    quarters = []
    for q in range(4):
        parts = [rows_ref[n * SLAB + 32 * q:n * SLAB + 32 * q + 32, CHANNELS:CHANNELS + HALF] for n in range(16)]
        quarters.append(jnp.concatenate(parts, axis=0))
    weight = jnp.concatenate(quarters, axis=1)
    copies = []
    for part in range(4):
        rows = pl.ds(part * 512, 512)
        projected = mm(rows_ref[rows, 0:CHANNELS], weight)
        keys = projected[:, :640]
        held_ref[rows, 0:640] = (keys * mm(head_factors(keys, sums, HEADS), spread)).astype(BF)
        held_ref[rows, 640:] = projected[:, 640:].astype(BF)
        copies.append(pltpu.make_async_copy(held_ref.at[rows], slab_ref.at[rows], out_sem.at[part]))
        copies[-1].start()
    for copy in copies:
        copy.wait()


def cross_kernel(ids_ref, yh_ref, lat_ref, mixed_ref, live_ref, a_ref, b_ref, slab_ref,
                 result_ref, held_ref, picked_ref, out_ref, co_ref, cq_ref, sem):
    arrivals = []
    for n in range(16):
        yh = yh_ref[0] if n < 8 else 1 - yh_ref[0]
        to = pl.multiple_of(yh * (8 * REST) + n % 8 * REST, REST)
        src = (a_ref, b_ref)[n // 8].at[pl.ds(n % 8 * SHARE, REST)]
        arrivals.append(pltpu.make_async_copy(src, held_ref.at[pl.ds(to, REST)], sem.at[24 + n]))
        arrivals[-1].start()
    blocks = []
    for n in range(24):
        block = pl.ds(pl.multiple_of(ids_ref[n // 8, n % 8] * 64, 64), 64)
        blocks.append(pltpu.make_async_copy(slab_ref.at[block], picked_ref.at[pl.ds(n * 64, 64)], sem.at[n]))
        blocks[-1].start()

    to, src = iota((192, 192), 0), iota((192, 192), 1)
    pick = onehot(src == (to % 64) // 8 * 24 + to // 64 * 8 + to % 8)
    mixed = jnp.concatenate([mm(pick, mixed_ref[at:at + 192, :]) for at in (0, 192)], axis=1).astype(BF)
    for copy in arrivals:
        copy.wait()
    for n in range(16):
        x, yh, c = n // 4, n // 2 % 2, n % 2
        at = (yh * 8 + x * 2 + c) * REST
        to = slice(n * 36, n * 36 + 36)
        out_ref[to, 0:PACK] = held_ref[at:at + 36, :]
        co_ref[to, 0:PACK] = held_ref[at + 36:at + 72, :]
        out_ref[to, PACK:] = held_ref[at + 72:at + 108, 0:256]
        co_ref[to, PACK:] = held_ref[at + 108:at + 144, 0:256]
        cq_ref[n * 72:n * 72 + 72, :] = held_ref[at + 72:at + 144, 256:256 + INNER]
    hidden = (lat_ref[...].astype(F32) + mm(mixed, out_ref[...])).astype(BF)
    normed = rms_rows(hidden.astype(F32)).astype(BF)
    query = head_normalize(mm(normed, cq_ref[...]))
    query = jnp.concatenate([query, jnp.zeros((192, 64), F32)], axis=1)
    head = iota((64, 640), 1) // HEAD
    value_head = (iota((64, 640), 1) - 64 + HEAD) // HEAD - 1
    crossed = []
    for tile in range(3):
        for copy in blocks[tile * 8:tile * 8 + 8]:
            copy.wait()
        rows = query[tile * 64:tile * 64 + 64]
        masked = jnp.concatenate([jnp.where(head == h, rows, 0.0).astype(BF) for h in range(HEADS)], axis=0)
        keys = slice(tile * 512, tile * 512 + 512)
        scores = mm_nt(masked, picked_ref[keys, 0:640]) * SCALE
        exponent = jnp.exp(scores) * live_ref[tile:tile + 1, :]
        weights = (exponent * (1.0 / jnp.sum(exponent, axis=-1, keepdims=True))).astype(BF)
        mixed = mm(weights, picked_ref[keys, 512:WIDTH])
        total = mixed[:64]
        for h in range(1, HEADS):
            total = jnp.where(value_head == h, mixed[h * 64:h * 64 + 64], total)
        crossed.append(total)
    crossed = jnp.concatenate(crossed, axis=0)[:, 64:].astype(BF)
    result_ref[...] = (hidden.astype(F32) + mm(crossed, co_ref[...])).astype(BF)


def call(kernel, shapes, count, scalars=(), hbm=(), out_hbm=False, scratch=(), us=1, vmem=60):
    memory = [pltpu.SMEM if n in scalars else pl.ANY if n in hbm else pltpu.VMEM for n in range(count)]
    out_memory = pl.ANY if out_hbm else pltpu.VMEM
    return pl.pallas_call(
        kernel,
        out_shape=shapes,
        in_specs=[pl.BlockSpec(memory_space=m) for m in memory],
        out_specs=jax.tree.map(lambda _: pl.BlockSpec(memory_space=out_memory), shapes),
        scratch_shapes=scratch,
        compiler_params=pltpu.CompilerParams(vmem_limit_bytes=vmem * 1024 * 1024),
        cost_estimate=pl.CostEstimate(flops=us * 1150000000, bytes_accessed=us * 1000000, transcendentals=0),
    )


def after(values, *others):
    count = len(values)
    return lax.optimization_barrier(tuple(values) + others)[:count]


SWAP = [(0, 1), (1, 0)]
STEPS = (0, 1, 3, 2)


def along_x(block):
    return [block] + [lax.ppermute(block, "x", [(i, (i + s) % 4) for i in range(4)]) for s in STEPS[1:]]


def across_core(blocks):
    stacked = jnp.stack(blocks)
    return stacked, lax.ppermute(stacked, "c", SWAP)


def places(device, rows, pad):
    place = jnp.arange(2 * pad, dtype=jnp.int32)
    side, row = place // pad, place % pad
    x, yh, c = device(side, row // rows)
    start = ((x * 2 + yh) * 2 + c) * rows
    return jnp.where(row < 8 * rows, start + row % rows, -1).reshape(1, 2 * pad)


def shards(latents, block_mask, occupancy, temporal_qkv, temporal_out, cross_query, cross_keyval, cross_out):
    x, yh, c, l = (lax.axis_index(name) for name in ("x", "yh", "c", "l"))
    shape = jax.ShapeDtypeStruct
    lat = latents.reshape(192, WIDTH)

    def by_step(side, j):
        return (x - jnp.array(STEPS, jnp.int32)[jnp.minimum(j // 2, 3)] + 4) % 4, yh ^ (j % 2), c ^ side

    share = call(share_kernel, shape((SHARE, PACK), BF), 5, us=2)(
        occupancy.reshape(128, CHANNELS), cross_keyval, cross_query, temporal_out, cross_out
    )
    far, qkv, sent = call(
        send_kernel,
        (shape((72, 3 * HALF), BF), shape((72, 3 * HALF), BF), shape((384, WIDTH), BF)),
        3, scalars=(0,), us=2,
    )(l.reshape(1).astype(jnp.int32), temporal_qkv, lat)

    def swap(block):
        return lax.ppermute(block, ("yh", "g", "l"), [(y, 7 - y) for y in range(8)])

    qkv_swapped, share_swapped = swap(far), swap(share)
    share_a = lax.all_gather(share, ("x", "c"), axis=0, tiled=True)
    time_rows = lax.all_to_all(
        sent.reshape(16, 24, WIDTH), ("l", "z"), split_axis=0, concat_axis=0, tiled=True
    ).reshape(384, WIDTH)
    own_blocks = along_x(qkv)
    share_swapped, qkv_swapped = after((share_swapped, qkv_swapped), time_rows, *own_blocks)
    normed = call(prep_kernel, shape((384, 1280), BF), 2, us=3, vmem=24)(time_rows, places(by_step, 72, 640))
    share_b = lax.all_gather(share_swapped, ("x", "c"), axis=0, tiled=True)
    pairs = zip(own_blocks, along_x(qkv_swapped))
    qkv_own, qkv_other = across_core([block for pair in pairs for block in pair])
    mixed = call(temporal_kernel, shape((384, HALF), BF), 3, us=5, vmem=24)(
        normed, qkv_own.reshape(INNER, 3 * HALF), qkv_other.reshape(INNER, 3 * HALF)
    )
    mixed_home = lax.all_to_all(
        mixed.reshape(16, 24, HALF), ("l", "z"), split_axis=0, concat_axis=0, tiled=True
    ).reshape(384, HALF)

    mask = block_mask[:, 0, :]
    rank = jnp.cumsum(mask, axis=1) - 1
    block = jnp.arange(32, dtype=jnp.int32)
    chosen = (rank[:, :, None] == jnp.arange(8, dtype=jnp.int32)) & (mask[:, :, None] > 0)
    ids = jnp.sum(jnp.where(chosen, block[None, :, None], 0), axis=1).astype(jnp.int32)
    live = jnp.repeat(jnp.any(chosen, axis=1), 64, axis=1).astype(F32)

    y_hi = yh.reshape(1).astype(jnp.int32)
    keys_values = call(
        slab_kernel, shape((2048, WIDTH), BF), 3, scalars=(0,), hbm=(1, 2), out_hbm=True, us=10,
        scratch=[
            pltpu.VMEM((2048, PACK), BF),
            pltpu.VMEM((2048, WIDTH), BF),
            pltpu.SemaphoreType.DMA((16,)),
            pltpu.SemaphoreType.DMA((4,)),
        ],
    )(y_hi, share_a, share_b)
    result = call(
        cross_kernel, shape((192, WIDTH), BF), 8, scalars=(0, 1), hbm=(5, 6, 7), us=10,
        scratch=[
            pltpu.VMEM((16 * REST, PACK), BF),
            pltpu.VMEM((24 * 64, WIDTH), BF),
            pltpu.VMEM((INNER, WIDTH), BF),
            pltpu.VMEM((INNER, WIDTH), BF),
            pltpu.VMEM((WIDTH, INNER), BF),
            pltpu.SemaphoreType.DMA((40,)),
        ],
    )(ids, y_hi, lat, mixed_home, live, share_a, share_b, keys_values)
    return result.reshape(latents.shape)


def solution(mesh):
    split = Mesh(mesh.devices.reshape(4, 2, 2, 2, 2, 8), ("x", "yh", "c", "g", "l", "z"))
    vox, vf = ("x", "yh", "c"), ("g", "l", "z")
    return jax.shard_map(
        shards,
        mesh=split,
        in_specs=(
            P(vf, vox, None),
            P(vf, vox, None),
            P(vox, None, None),
            P(vox, None),
            P(vox, None),
            P(vox, None),
            P(vox, None),
            P(vox, None),
        ),
        out_specs=P(vf, vox, None),
        check_vma=False,
    )
```
